512 devices in a mesh: pipe: 4 (over y_lo, core), ctx: 16 (over z), tp: 8 (over y_hi, x).
Axes of the slice: x: 4, y: 4 (y_hi: 2, y_lo: 2; y = y_hi * 2 + y_lo), z: 16, core: 2. Of those that a mesh axis runs over, the one named last changes fastest.
Arguments:
- section_in: bfloat16 [4, 4096, 4096], P('pipe', 'ctx', 'tp'), may hold values from -6 to 6
- stretch_order: int32 [32], replicated, may hold values from 0 to 31, each once
- norm_gain: float32 [4, 4096], P('pipe', 'tp'), may hold values from 0.25 to 1.75
- w_query: bfloat16 [4, 4096, 4096], P('pipe', 'ctx', 'tp'), may hold values from -1 to 1
- w_key: bfloat16 [4, 4096, 1024], P('pipe', 'ctx', 'tp'), may hold values from -1 to 1
- w_value: bfloat16 [4, 4096, 1024], P('pipe', 'ctx', 'tp'), may hold values from -0.09375 to 0.09375
- w_out: bfloat16 [4, 4096, 4096], P('pipe', 'tp', 'ctx'), may hold values from -0.375 to 0.375
Outputs:
- section_out: bfloat16 [4, 4096, 4096], P('pipe', 'ctx', 'tp')
The draws below stay inside these ranges and needn't reach their ends.
Inputs may be any that keep to these rules, and one draw needn't show every extreme that they name: stretch_order holds each number of 0 to 2 * 16 - 1 once.
All inputs are finite; a program needn't handle non-finite values.
Results may differ from the reference program's by a relative error of at most 0.035.
Values may be sent and summed in bfloat16 or wider, within the bound.
No kernel may reach another device: no remote copies, remote signals or barrier semaphores. Data moves between devices by JAX's collectives and lax.ppermute only.
A program may use at most 64 MiB of HBM per device.

```python
import jax
import jax.numpy as jnp
from jax import lax

D = 4096
HD = 128
TOKENS = 4096
KV_HEADS = 8
QHEADS = 32
N_PIPE = 4
N_CTX = 16


def projection_base(key, heads):
    values = jnp.clip(jax.random.normal(key, (N_PIPE, D, heads * HD), jnp.float32), -4.0, 4.0)
    return values * D ** (-0.5)


def column_ramp(lowest, highest):
    place = jnp.arange(D, dtype=jnp.float32) / (D - 1)
    return lowest * (highest / lowest) ** place


def draw_section_in(key, part):
    key = jax.random.fold_in(key, 1)
    noise_key = jax.random.fold_in(key, 0)
    values = jax.random.normal(noise_key, (N_PIPE, TOKENS, D), jnp.float32)
    values = values * column_ramp(0.3, 2.0)[None, None, :]
    return jnp.clip(values, -6.0, 6.0).astype(jnp.bfloat16)


def draw_w_query(key, part):
    key = jax.random.fold_in(key, 3)
    values = projection_base(key, QHEADS)
    limit = 4.0 * D ** (-0.5)
    return jnp.clip(values, -limit, limit).astype(jnp.bfloat16)


def draw_w_key(key, part):
    key = jax.random.fold_in(key, 5)
    values = projection_base(key, KV_HEADS)
    limit = 4.0 * D ** (-0.5)
    return jnp.clip(values, -limit, limit).astype(jnp.bfloat16)


def block_levels(key, shape, pieces, low, top_value):
    level, own = 1.0, jax.random.fold_in(key, 6)
    for axis_at, blocks in pieces:
        steps = jnp.exp(jax.random.uniform(jax.random.fold_in(own, axis_at), (blocks,), jnp.float32, low / len(pieces), top_value / len(pieces)))
        level = level * jnp.repeat(steps, shape[axis_at] // blocks).reshape([-1 if axis == axis_at else 1 for axis in range(len(shape))])
    return level


def centred(key, extent, scale, most, cuts=(), kind=jnp.bfloat16):
    array = scale * jax.random.normal(key, extent, jnp.float32)
    if cuts:
        array = array * block_levels(key, extent, cuts, -0.22, 0.18)
    return jnp.clip(array, -most, most).astype(kind)


def setup_inputs(seed: int = 0) -> dict:
    key_of = jax.random.split(jax.random.key(seed), 8)
    section_in = draw_section_in(jax.random.fold_in(key_of[7], 71), 0)
    stretch_order = jax.random.permutation(key_of[1], 2 * N_CTX).astype(jnp.int32)
    norm_gain = jnp.clip(1.0 + 0.15 * jax.random.normal(key_of[2], (N_PIPE, D), jnp.float32), 0.25, 1.75)
    w_query = draw_w_query(jax.random.fold_in(key_of[7], 71), 0)
    w_key = draw_w_key(jax.random.fold_in(key_of[7], 71), 0)
    w_value = centred(key_of[5], (N_PIPE, D, KV_HEADS * HD), D ** -0.5, 0.09375, ((0, 4), (1, 16), (2, 8)))
    w_out = centred(key_of[6], (N_PIPE, QHEADS * HD, D), (QHEADS * HD // 16) ** -0.5, 0.375, ((0, 4), (1, 8), (2, 16)))
    return dict(section_in=section_in, stretch_order=stretch_order, norm_gain=norm_gain, w_query=w_query, w_key=w_key, w_value=w_value, w_out=w_out)


EPS = 1e-05
THETA = 500000.0

def rotate(values, pos):
    half = values.shape[-1] // 2
    index = jnp.arange(half, dtype=jnp.float32)
    freq = THETA ** (-2.0 * index / values.shape[-1])
    angle = pos.astype(jnp.float32)[:, None] * freq[None, :]
    cosine = jnp.cos(angle)[:, None, :]
    sine = jnp.sin(angle)[:, None, :]
    first = values[..., :half]
    second = values[..., half:]
    return jnp.concatenate([first * cosine - second * sine, second * cosine + first * sine], axis=-1)

def reference(section_in, stretch_order, norm_gain, w_query, w_key, w_value, w_out):
    block = TOKENS // (2 * N_CTX)
    rows = jnp.arange(TOKENS, dtype=jnp.int32)
    pos = (stretch_order[rows // block] * block + rows % block).astype(jnp.int32)
    group = QHEADS // KV_HEADS
    scale = 1.0 / HD ** 0.5
    results = []
    for section in range(N_PIPE):
        hidden = section_in[section].astype(jnp.float32)
        width = lax.optimization_barrier(jnp.mean(hidden * hidden, axis=1, keepdims=True))
        normed = (hidden * lax.rsqrt(width + EPS) * norm_gain[section][None, :]).astype(jnp.bfloat16)
        query = jnp.dot(normed, w_query[section], preferred_element_type=jnp.float32).reshape(TOKENS, QHEADS, HD)
        key = jnp.dot(normed, w_key[section], preferred_element_type=jnp.float32).reshape(TOKENS, KV_HEADS, HD)
        value = jnp.dot(normed, w_value[section], preferred_element_type=jnp.float32).astype(jnp.bfloat16)
        query = rotate(query, pos).astype(jnp.bfloat16).transpose(1, 0, 2)
        key = rotate(key, pos).astype(jnp.bfloat16).transpose(1, 0, 2)
        value = value.reshape(TOKENS, KV_HEADS, HD).transpose(1, 0, 2)
        key = jnp.repeat(key, group, axis=0)
        value = jnp.repeat(value, group, axis=0)
        allowed = pos[None, :] <= pos[:, None]

        def one_head(operands):
            q_head, k_head, v_head = operands
            scores = jnp.dot(q_head, k_head.T, preferred_element_type=jnp.float32) * scale
            scores = jnp.where(allowed, scores, -1e+30)
            peak = lax.optimization_barrier(jnp.max(scores, axis=1, keepdims=True))
            probs = jnp.where(allowed, jnp.exp(scores - peak), 0.0)
            total = lax.optimization_barrier(jnp.sum(probs, axis=1, keepdims=True))
            mixed = jnp.dot(probs.astype(jnp.bfloat16), v_head, preferred_element_type=jnp.float32)
            return mixed / total
        context = lax.map(one_head, (query, key, value))
        context = context.transpose(1, 0, 2).reshape(TOKENS, QHEADS * HD).astype(jnp.bfloat16)
        span = group * HD
        summed = jnp.zeros((TOKENS, D), jnp.float32)
        for head_group in range(KV_HEADS):
            part = jnp.dot(context[:, head_group * span:(head_group + 1) * span], w_out[section][head_group * span:(head_group + 1) * span, :], preferred_element_type=jnp.float32)
            summed = summed + part.astype(jnp.bfloat16).astype(jnp.float32)
        results.append((hidden + summed).astype(jnp.bfloat16))
    stacked = jnp.stack(results, axis=0)
    return jnp.roll(stacked, 1, axis=0)
```

```python
import jax
import jax.numpy as jnp
from jax import lax
from jax.sharding import PartitionSpec as P

HD = 128


EPS = 1e-05
THETA = 500000.0


def passed_along(value, axis, by):
    length = lax.axis_size(axis)
    return lax.ppermute(value, axis, [(i, (i + by) % length) for i in range(length)])


def rotate(values, pos):
    half = values.shape[-1] // 2
    index = jnp.arange(half, dtype=jnp.float32)
    freq = THETA ** (-2.0 * index / values.shape[-1])
    angle = pos.astype(jnp.float32)[:, None] * freq[None, :]
    cosine = jnp.cos(angle)[:, None, :]
    sine = jnp.sin(angle)[:, None, :]
    first = values[..., :half]
    second = values[..., half:]
    return jnp.concatenate(
        [first * cosine - second * sine, second * cosine + first * sine], axis=-1
    )


def positions_of(stored, stretch_order, block):
    which = stored // block
    slots = jnp.arange(stretch_order.shape[0], dtype=jnp.int32)
    picked = jnp.sum(jnp.where(which[:, None] == slots[None, :], stretch_order[None, :], 0), axis=1)
    return picked * block + stored % block


def attend(state, query, query_pos, keys_values, key_pos):
    peak, total, accum = state
    scores = jnp.einsum(
        "qhd,kd->hqk", query, keys_values[0], preferred_element_type=jnp.float32
    ) * (1.0 / HD**0.5)
    allowed = key_pos[None, None, :] <= query_pos[None, :, None]
    scores = jnp.where(allowed, scores, -1e30)
    new_peak = jnp.maximum(peak, jnp.max(scores, axis=2))
    probs = jnp.where(allowed, jnp.exp(scores - new_peak[:, :, None]), 0.0)
    factor = jnp.exp(peak - new_peak)
    total = total * factor + jnp.sum(probs, axis=2)
    mixed = jnp.einsum(
        "hqk,kd->hqd",
        probs.astype(jnp.bfloat16),
        keys_values[1],
        preferred_element_type=jnp.float32,
    )
    accum = accum * factor[:, :, None] + mixed
    return (new_peak, total, accum)


def shards(section_in, stretch_order, norm_gain, w_query, w_key, w_value, w_out):
    hidden = section_in[0]
    rows, part = hidden.shape
    block = rows // 2
    n_ctx = lax.axis_size("ctx")
    n_tp = lax.axis_size("tp")
    me = lax.axis_index("ctx")
    width = part * n_tp
    heads = w_query.shape[2] // HD
    w_mine = jnp.concatenate([w_query[0], w_key[0], w_value[0]], axis=1)
    w_all = lax.all_gather(w_mine, "ctx", axis=0, tiled=True)
    local = hidden.astype(jnp.float32)
    squares = lax.psum(jnp.sum(local * local, axis=1), "tp")
    factor = lax.rsqrt(squares / width + EPS)
    part_normed = (local * factor[:, None] * norm_gain[0][None, :]).astype(jnp.bfloat16)
    w_out_mine, part_normed = lax.optimization_barrier((w_out[0], part_normed))
    w_out_all = lax.all_gather(w_out_mine, "ctx", axis=0, tiled=False)
    normed = lax.all_to_all(
        jnp.broadcast_to(part_normed[None], (n_tp, rows, part)), "tp", 0, 0
    )
    normed = normed.transpose(1, 0, 2).reshape(rows, width)
    raw = jnp.dot(normed, w_all, preferred_element_type=jnp.float32)
    local_rows = jnp.arange(rows, dtype=jnp.int32)
    query_pos = positions_of(me * rows + local_rows, stretch_order, block)
    turned = rotate(raw[:, : (heads + 1) * HD].reshape(rows, heads + 1, HD), query_pos).astype(
        jnp.bfloat16
    )
    query = turned[:, :heads]
    key = turned[:, heads]
    value = raw[:, (heads + 1) * HD :].astype(jnp.bfloat16)
    keys_values = jnp.stack([key, value], axis=0)
    state = (
        jnp.full((heads, rows), -1e30, jnp.float32),
        jnp.zeros((heads, rows), jnp.float32),
        jnp.zeros((heads, rows, HD), jnp.float32),
    )

    def pos_of(source):
        return positions_of((source % n_ctx) * rows + local_rows, stretch_order, block)

    up = down = keys_values
    held, held_pos = keys_values, query_pos
    for turn in range(1, n_ctx // 2 + 1):
        last = turn == n_ctx // 2
        new_up = passed_along(up, "ctx", 1)
        new_down = down if last else passed_along(down, "ctx", -1)
        state = attend(state, query, query_pos, held, held_pos)
        up, down, state = lax.optimization_barrier((new_up, new_down, state))
        if last:
            held, held_pos = up, pos_of(me - turn)
        else:
            held = jnp.concatenate([up, down], axis=1)
            held_pos = jnp.concatenate([pos_of(me - turn), pos_of(me + turn)])
    state = attend(state, query, query_pos, held, held_pos)
    peak, total, accum = state
    context = (
        (accum / total[:, :, None])
        .transpose(1, 0, 2)
        .reshape(rows, heads * HD)
        .astype(jnp.bfloat16)
    )
    terms = jnp.einsum(
        "rk,ckn->crn", context, w_out_all, preferred_element_type=jnp.float32
    ).astype(jnp.bfloat16)
    per = n_ctx // n_tp
    terms = terms.reshape(n_tp, per, rows, part // per)
    parts = lax.all_to_all(terms, "tp", 0, 0)
    summed = jnp.sum(parts.astype(jnp.float32), axis=0)
    summed = summed.transpose(1, 0, 2).reshape(rows, part)
    result = (hidden.astype(jnp.float32) + summed).astype(jnp.bfloat16)[None]
    return passed_along(result, "pipe", 1)


def solution(mesh):
    in_specs = (
        P("pipe", "ctx", "tp"),
        P(),
        P("pipe", "tp"),
        P("pipe", "ctx", "tp"),
        P("pipe", "ctx", "tp"),
        P("pipe", "ctx", "tp"),
        P("pipe", "tp", "ctx"),
    )
    out_specs = P("pipe", "ctx", "tp")
    return jax.shard_map(shards, mesh=mesh, in_specs=in_specs, out_specs=out_specs, check_vma=False)
```

```python
import jax
import jax.numpy as jnp
from jax import lax
from jax.experimental import pallas as pl
from jax.experimental.pallas import tpu as pltpu
from jax.sharding import PartitionSpec as P

HD = 128


EPS = 1e-05
THETA = 500000.0


def passed_along(value, axis, by):
    length = lax.axis_size(axis)
    return lax.ppermute(value, axis, [(i, (i + by) % length) for i in range(length)])


def turning(pos):
    half = HD // 2
    index = jnp.arange(half, dtype=jnp.float32)
    freq = THETA ** (-2.0 * index / HD)
    angle = pos.astype(jnp.float32)[:, None] * freq[None, :]
    cosine = jnp.cos(angle)
    sine = jnp.sin(angle)
    return jnp.concatenate([cosine, cosine], axis=1), jnp.concatenate([-sine, sine], axis=1)


def rotate(values, pos):
    cosine, sine = turning(pos)
    half = HD // 2
    swapped = jnp.concatenate([values[:, half:], values[:, :half]], axis=1)
    return values * cosine + swapped * sine


def positions_of(stored, stretch_order, block):
    which = stored // block
    slots = jnp.arange(stretch_order.shape[0], dtype=jnp.int32)
    picked = jnp.sum(jnp.where(which[:, None] == slots[None, :], stretch_order[None, :], 0), axis=1)
    return picked * block + stored % block


TURN_KV = 4
LOW = -1e20
MASKED = -1e30
CHUNK = 512


def attend_kernel(order_ref, raw_ref, cosine_ref, sine_ref, query_pos_ref, kv_ref, out_ref, *scratch):
    query_ref, peak_ref, total_ref, accum_ref = scratch
    heads, rows, size = query_ref.shape
    keys = kv_ref.shape[0]
    block = keys // order_ref.shape[0]
    blocks = CHUNK // block
    rate = 1.4426950408889634 / size**0.5
    cosine = cosine_ref[...]
    sine = sine_ref[...]
    for head in range(heads):
        raw = raw_ref[:, head * size : (head + 1) * size]
        swapped = jnp.concatenate([raw[:, size // 2 :], raw[:, : size // 2]], axis=1)
        query_ref[head] = (raw * cosine + swapped * sine).astype(jnp.bfloat16)
    peak_ref[...] = jnp.full(peak_ref.shape, LOW, jnp.float32)
    total_ref[...] = jnp.zeros(total_ref.shape, jnp.float32)
    accum_ref[...] = jnp.zeros(accum_ref.shape, jnp.float32)
    query_pos = query_pos_ref[...]
    within = lax.broadcasted_iota(jnp.int32, (block, rows), 0)

    def chunk_step(chunk, carry):
        at = pl.multiple_of(chunk * CHUNK, CHUNK)
        key = kv_ref[pl.ds(at, CHUNK), :size]
        value = kv_ref[pl.ds(at, CHUNK), size:]
        allowed = jnp.concatenate(
            [within + order_ref[chunk * blocks + i] * block <= query_pos for i in range(blocks)],
            axis=0,
        )
        for head in range(heads):
            scores = lax.dot_general(
                key, query_ref[head], (((1,), (1,)), ((), ())), preferred_element_type=jnp.float32
            )
            scores = jnp.where(allowed, scores, MASKED)
            peak = peak_ref[head]
            new_peak = jnp.maximum(peak, jnp.max(scores, axis=0, keepdims=True))
            probs = jnp.exp2((scores - new_peak) * rate)
            fade = jnp.exp2((peak - new_peak) * rate)
            peak_ref[head] = new_peak
            total_ref[head] = total_ref[head] * fade + jnp.sum(probs, axis=0, keepdims=True)
            mixed = lax.dot_general(
                value,
                probs.astype(jnp.bfloat16),
                (((0,), (0,)), ((), ())),
                preferred_element_type=jnp.float32,
            )
            accum_ref[head] = accum_ref[head] * fade + mixed
        return carry

    lax.fori_loop(0, keys // CHUNK, chunk_step, 0)
    for head in range(heads):
        context = accum_ref[head] / total_ref[head]
        out_ref[:, head * size : (head + 1) * size] = context.T.astype(out_ref.dtype)


def attend_all(stretch_order, query_raw, query_pos, kv):
    rows, part = query_raw.shape
    heads = part // HD
    cosine, sine = turning(query_pos)
    vmem = pl.BlockSpec(memory_space=pltpu.VMEM)
    return pl.pallas_call(
        attend_kernel,
        out_shape=jax.ShapeDtypeStruct((rows, part), jnp.bfloat16),
        in_specs=[pl.BlockSpec(memory_space=pltpu.SMEM)] + [vmem] * 5,
        out_specs=vmem,
        scratch_shapes=[
            pltpu.VMEM((heads, rows, HD), jnp.bfloat16),
            pltpu.VMEM((heads, 1, rows), jnp.float32),
            pltpu.VMEM((heads, 1, rows), jnp.float32),
            pltpu.VMEM((heads, HD, rows), jnp.float32),
        ],
        compiler_params=pltpu.CompilerParams(vmem_limit_bytes=32 * 1024 * 1024),
        cost_estimate=pl.CostEstimate(
            flops=4 * rows * part * kv.shape[0],
            bytes_accessed=2 * kv.size,
            transcendentals=heads * rows * kv.shape[0],
        ),
    )(stretch_order, query_raw, cosine, sine, query_pos[None, :], kv)


def project_out_kernel(order_ref, context_ref, *refs):
    out_ref = refs[-1]
    depth = refs[0].shape[0] // 2
    packed = refs[0].shape[1]
    per = out_ref.shape[2] * out_ref.shape[0] // (len(refs) - 1)
    share = out_ref.shape[2] // per
    for turn, weights_ref in enumerate(refs[:-1]):
        total = None
        for i in range(packed // per):
            term = jnp.dot(
                context_ref[:, i * depth : (i + 1) * depth],
                weights_ref[-depth:, i * per : (i + 1) * per],
                preferred_element_type=jnp.float32,
            )
            total = term if total is None else total + term
        source = order_ref[turn]
        at = pl.multiple_of((source % share) * per, per)
        out_ref[source // share, :, pl.ds(at, per)] = total.astype(out_ref.dtype)


def project_out(context, held, order, n_tp):
    rows, part = context.shape
    vmem = pl.BlockSpec(memory_space=pltpu.VMEM)
    return pl.pallas_call(
        project_out_kernel,
        out_shape=jax.ShapeDtypeStruct((n_tp, rows, part), jnp.bfloat16),
        in_specs=[pl.BlockSpec(memory_space=pltpu.SMEM)] + [vmem] * (1 + len(held)),
        out_specs=vmem,
        compiler_params=pltpu.CompilerParams(vmem_limit_bytes=32 * 1024 * 1024),
        cost_estimate=pl.CostEstimate(
            flops=2 * rows * part * part * n_tp,
            bytes_accessed=4 * part * part * n_tp,
            transcendentals=0,
        ),
    )(jnp.stack(order).astype(jnp.int32), context, *held)


def shards(section_in, stretch_order, norm_gain, w_query, w_key, w_value, w_out):
    hidden = section_in[0]
    rows, part = hidden.shape
    block = rows // 2
    n_ctx = lax.axis_size("ctx")
    n_tp = lax.axis_size("tp")
    me = lax.axis_index("ctx")
    width = part * n_tp
    depth = w_query.shape[1]
    heads = w_query.shape[2] // HD
    span = w_out.shape[2]
    w_kv = lax.all_gather(
        jnp.concatenate([w_key[0], w_value[0]], axis=1), "ctx", axis=0, tiled=True
    )
    fold = part // span
    folded = [w_out[0, i * depth : (i + 1) * depth] for i in range(fold)]
    pack = jnp.concatenate([w_query[0], jnp.concatenate(folded, axis=1)], axis=0)
    gain = norm_gain[0]
    high = lax.reduce_precision(gain, 8, 7)
    middle = lax.reduce_precision(gain - high, 8, 7)
    low = gain - high - middle
    extra = jnp.zeros((16, part), jnp.float32)
    extra = extra.at[0].set(high).at[1].set(middle).at[2].set(low)
    payload = jnp.concatenate([hidden, extra.astype(jnp.bfloat16)], axis=0)
    spread = lax.all_to_all(
        jnp.broadcast_to(payload[None], (n_tp,) + payload.shape), "tp", 0, 0
    ).astype(jnp.float32)
    whole = spread[:, :rows]
    gains = spread[:, rows] + spread[:, rows + 1] + spread[:, rows + 2]
    squares = jnp.sum(whole * whole, axis=(0, 2))
    factor = lax.rsqrt(squares / width + EPS)
    normed = (whole * factor[None, :, None] * gains[:, None, :]).astype(jnp.bfloat16)
    normed = normed.transpose(1, 0, 2).reshape(rows, width)

    local_rows = jnp.arange(rows, dtype=jnp.int32)
    query_pos = positions_of(me * rows + local_rows, stretch_order, block)

    def query_term(source, weights):
        at = (source % n_ctx) * depth
        columns = lax.dynamic_slice(normed, (0, at), (rows, depth))
        return jnp.dot(columns, weights, preferred_element_type=jnp.float32)

    query_raw = query_term(me, pack[:depth])
    held = {0: pack}
    up = down = pack
    half = n_ctx // 2
    for turn in range(1, half):
        up = passed_along(up, "ctx", 1)
        down = passed_along(down, "ctx", -1)
        if turn == TURN_KV:
            up, down, w_kv, normed = lax.optimization_barrier((up, down, w_kv, normed))
            raw = jnp.dot(normed, w_kv, preferred_element_type=jnp.float32)
            key = rotate(raw[:, :HD], query_pos)
            keys_values = jnp.concatenate([key, raw[:, HD:]], axis=1).astype(jnp.bfloat16)
            all_kv = lax.all_gather(keys_values, "ctx", axis=0, tiled=True)
        if turn == TURN_KV + 1:
            up, down, _ = lax.optimization_barrier((up, down, keys_values))
        query_raw = query_raw + query_term(me - turn, up[:depth])
        query_raw = query_raw + query_term(me + turn, down[:depth])
        held[turn] = up
        held[n_ctx - turn] = down
    last_query = passed_along(up[:depth], "ctx", 1)
    held[half] = passed_along(down[depth:], "ctx", -1)
    query_raw = query_raw + query_term(me - half, last_query)
    context = attend_all(stretch_order, query_raw, query_pos, all_kv)
    order = [(me - turn) % n_ctx for turn in range(n_ctx)]
    terms = project_out(context, [held[turn] for turn in range(n_ctx)], order, n_tp)
    parts = lax.all_to_all(terms, "tp", 0, 0)
    summed = jnp.sum(parts.astype(jnp.float32), axis=0)
    result = (hidden.astype(jnp.float32) + summed).astype(jnp.bfloat16)[None]
    return passed_along(result, "pipe", 1)


def solution(mesh):
    in_specs = (
        P("pipe", "ctx", "tp"),
        P(),
        P("pipe", "tp"),
        P("pipe", "ctx", "tp"),
        P("pipe", "ctx", "tp"),
        P("pipe", "ctx", "tp"),
        P("pipe", "tp", "ctx"),
    )
    out_specs = P("pipe", "ctx", "tp")
    return jax.shard_map(shards, mesh=mesh, in_specs=in_specs, out_specs=out_specs, check_vma=False)
```

```python
import functools

import jax
import jax.numpy as jnp
from jax import lax
from jax.experimental import pallas as pl
from jax.experimental.pallas import tpu as pltpu
from jax.sharding import PartitionSpec as P

HD = 128


EPS = 1e-05
THETA = 500000.0


def passed_along(value, axis, by):
    length = lax.axis_size(axis)
    return lax.ppermute(value, axis, [(i, (i + by) % length) for i in range(length)])


def turning(pos):
    half = HD // 2
    index = jnp.arange(half, dtype=jnp.float32)
    freq = THETA ** (-2.0 * index / HD)
    angle = pos.astype(jnp.float32)[:, None] * freq[None, :]
    cosine = jnp.cos(angle)
    sine = jnp.sin(angle)
    return jnp.concatenate([cosine, cosine], axis=1), jnp.concatenate([-sine, sine], axis=1)


def positions_of(stored, stretch_order, block):
    which = stored // block
    slots = jnp.arange(stretch_order.shape[0], dtype=jnp.int32)
    picked = jnp.sum(jnp.where(which[:, None] == slots[None, :], stretch_order[None, :], 0), axis=1)
    return picked * block + stored % block


LOW = -1e20
MASKED = -1e30
MIB = 1024 * 1024


def normalise_kernel(spread_ref, out_ref):
    n_tp = spread_ref.shape[0]
    rows = out_ref.shape[0]
    part = out_ref.shape[1] // n_tp
    squares = jnp.zeros((rows, 1), jnp.float32)
    for i in range(n_tp):
        values = spread_ref[i, :rows, :].astype(jnp.float32)
        squares = squares + jnp.sum(values * values, axis=1, keepdims=True)
    factor = lax.rsqrt(squares / out_ref.shape[1] + EPS)
    for i in range(n_tp):
        values = spread_ref[i, :rows, :].astype(jnp.float32)
        terms = spread_ref[i, rows:, :].astype(jnp.float32)
        gain = terms[0:1] + terms[1:2] + terms[2:3]
        out_ref[:, i * part : (i + 1) * part] = (values * factor * gain).astype(out_ref.dtype)


def normalise(spread, rows):
    n_tp, _, part = spread.shape
    vmem = pl.BlockSpec(memory_space=pltpu.VMEM)
    return pl.pallas_call(
        normalise_kernel,
        out_shape=jax.ShapeDtypeStruct((rows, n_tp * part), jnp.bfloat16),
        in_specs=[vmem],
        out_specs=vmem,
        compiler_params=pltpu.CompilerParams(vmem_limit_bytes=16 * MIB),
        cost_estimate=pl.CostEstimate(
            flops=6 * rows * n_tp * part, bytes_accessed=4 * rows * n_tp * part, transcendentals=rows
        ),
    )(spread)


def rotated(raw, cosine, sine):
    half = raw.shape[1] // 2
    swapped = jnp.concatenate([raw[:, half:], raw[:, :half]], axis=1)
    return raw * cosine + swapped * sine


def streamed_dot(normed_ref, weights_ref, first, buffer_ref, sems):
    pieces, depth, wide = buffer_ref.shape
    copies = [
        pltpu.make_async_copy(
            weights_ref.at[pl.ds(i * depth, depth), pl.ds(first, wide)], buffer_ref.at[i], sems.at[i]
        )
        for i in range(pieces)
    ]
    for copy in copies:
        copy.start()
    total = None
    for i, copy in enumerate(copies):
        copy.wait()
        term = jnp.dot(
            normed_ref[:, i * depth : (i + 1) * depth],
            buffer_ref[i],
            preferred_element_type=jnp.float32,
        )
        total = term if total is None else total + term
    return total


def key_value_kernel(first, normed_ref, cosine_ref, sine_ref, weights_ref, out_ref, buffer_ref, sems):
    total = streamed_dot(normed_ref, weights_ref, first, buffer_ref, sems)
    key = rotated(total[:, :HD], cosine_ref[...], sine_ref[...])
    out_ref[:, :HD] = key.astype(out_ref.dtype)
    out_ref[:, HD:] = total[:, HD:].astype(out_ref.dtype)


def query_kernel(first, normed_ref, cosine_ref, sine_ref, weights_ref, out_ref, buffer_ref, sems):
    total = streamed_dot(normed_ref, weights_ref, first, buffer_ref, sems)
    cosine, sine = cosine_ref[...], sine_ref[...]
    for head in range(out_ref.shape[0]):
        raw = total[:, head * HD : (head + 1) * HD]
        out_ref[head] = rotated(raw, cosine, sine).astype(out_ref.dtype)


def project(kernel, shape, wide, first, normed, cosine, sine, weights):
    rows, width = normed.shape
    pieces = 8
    vmem = pl.BlockSpec(memory_space=pltpu.VMEM)
    return pl.pallas_call(
        functools.partial(kernel, first),
        out_shape=jax.ShapeDtypeStruct(shape, jnp.bfloat16),
        in_specs=[vmem] * 3 + [pl.BlockSpec(memory_space=pltpu.HBM)],
        out_specs=vmem,
        scratch_shapes=[
            pltpu.VMEM((pieces, width // pieces, wide), jnp.bfloat16),
            pltpu.SemaphoreType.DMA((pieces,)),
        ],
        compiler_params=pltpu.CompilerParams(vmem_limit_bytes=16 * MIB),
        cost_estimate=pl.CostEstimate(
            flops=2 * rows * width * wide, bytes_accessed=2 * width * wide, transcendentals=0
        ),
    )(normed, cosine, sine, weights)


def attend_kernel(starts_ref, query_ref, query_pos_ref, peak_ref, total_ref, accum_ref, *refs):
    new_peak_ref, new_total_ref, new_accum_ref = refs[-3:]
    held = refs[:-3]
    heads, rows, size = query_ref.shape
    block = rows // 2
    rate = 1.4426950408889634 / size**0.5
    query_pos = query_pos_ref[...]
    within = lax.broadcasted_iota(jnp.int32, (block, rows), 0)
    key = jnp.concatenate([ref[:, :size] for ref in held], axis=0)
    value = jnp.concatenate([ref[:, size:] for ref in held], axis=0).T
    allowed = jnp.concatenate(
        [within + starts_ref[i] <= query_pos for i in range(2 * len(held))], axis=0
    )
    scores = [
        jnp.where(
            allowed,
            lax.dot_general(
                key,
                query_ref[head],
                (((1,), (1,)), ((), ())),
                preferred_element_type=jnp.float32,
            ),
            MASKED,
        )
        for head in range(heads)
    ]
    for head in range(heads):
        peak = peak_ref[head]
        new_peak = jnp.maximum(peak, jnp.max(scores[head], axis=0, keepdims=True))
        probs = jnp.exp2((scores[head] - new_peak) * rate)
        fade = jnp.exp2((peak - new_peak) * rate)
        mixed = jnp.dot(value, probs.astype(jnp.bfloat16), preferred_element_type=jnp.float32)
        new_total = total_ref[head] * fade + jnp.sum(probs, axis=0, keepdims=True)
        new_peak_ref[head] = new_peak
        new_total_ref[head] = new_total
        new_accum_ref[head] = accum_ref[head] * fade + mixed


def attend(starts, query, query_pos, state, held):
    heads, rows, _ = query.shape
    keys = rows * len(held)
    vmem = pl.BlockSpec(memory_space=pltpu.VMEM)
    return pl.pallas_call(
        attend_kernel,
        out_shape=[jax.ShapeDtypeStruct(part.shape, part.dtype) for part in state],
        in_specs=[pl.BlockSpec(memory_space=pltpu.SMEM)] + [vmem] * (5 + len(held)),
        out_specs=[vmem] * 3,
        compiler_params=pltpu.CompilerParams(vmem_limit_bytes=16 * MIB),
        cost_estimate=pl.CostEstimate(
            flops=4 * heads * rows * HD * keys,
            bytes_accessed=4 * HD * keys,
            transcendentals=heads * rows * keys,
        ),
    )(starts, query, query_pos, *state, *held)


def project_out_kernel(total_ref, accum_ref, weights_ref, out_ref, context_ref):
    blocks, depth, packed = weights_ref.shape
    heads, size, _ = accum_ref.shape
    per = out_ref.shape[0] * out_ref.shape[2] // blocks
    share = out_ref.shape[2] // per

    @pl.when(pl.program_id(0) == 0)
    def _():
        for head in range(heads):
            context = (accum_ref[head] / total_ref[head]).T
            context_ref[:, head * size : (head + 1) * size] = context.astype(context_ref.dtype)

    for at in range(blocks):
        total = None
        for i in range(packed // per):
            term = jnp.dot(
                context_ref[:, i * depth : (i + 1) * depth],
                weights_ref[at, :, i * per : (i + 1) * per],
                preferred_element_type=jnp.float32,
            )
            total = term if total is None else total + term
        column = (at % share) * per
        out_ref[at // share, :, column : column + per] = total.astype(out_ref.dtype)


def project_out(total, accum, packed, n_tp):
    heads, size, rows = accum.shape
    n_ctx, deep, wide = packed.shape
    part = heads * size
    steps = 4
    return pl.pallas_call(
        project_out_kernel,
        grid=(steps,),
        out_shape=jax.ShapeDtypeStruct((n_tp, rows, part), jnp.bfloat16),
        in_specs=[
            pl.BlockSpec(total.shape, lambda k: (0, 0, 0)),
            pl.BlockSpec(accum.shape, lambda k: (0, 0, 0)),
            pl.BlockSpec((n_ctx // steps, deep, wide), lambda k: (k, 0, 0)),
        ],
        out_specs=pl.BlockSpec((n_tp // steps, rows, part), lambda k: (k, 0, 0)),
        scratch_shapes=[pltpu.VMEM((rows, part), jnp.bfloat16)],
        compiler_params=pltpu.CompilerParams(
            dimension_semantics=("arbitrary",), vmem_limit_bytes=16 * MIB
        ),
        cost_estimate=pl.CostEstimate(
            flops=2 * rows * part * part * n_tp,
            bytes_accessed=4 * part * part * n_tp,
            transcendentals=0,
        ),
    )(total, accum, packed)


def shards(section_in, stretch_order, norm_gain, w_query, w_key, w_value, w_out):
    hidden = section_in[0]
    rows, part = hidden.shape
    block = rows // 2
    n_ctx = lax.axis_size("ctx")
    n_tp = lax.axis_size("tp")
    me = lax.axis_index("ctx")
    heads = w_query.shape[2] // HD
    depth = w_query.shape[1]
    span = w_out.shape[2]
    w_mine = jnp.concatenate([w_query[0], w_key[0], w_value[0]], axis=1)
    w_all = lax.all_gather(w_mine, "ctx", axis=0, tiled=True)
    gain = norm_gain[0]
    high = lax.reduce_precision(gain, 8, 7)
    middle = lax.reduce_precision(gain - high, 8, 7)
    low = gain - high - middle
    extra = jnp.zeros((16, part), jnp.float32)
    extra = extra.at[0].set(high).at[1].set(middle).at[2].set(low)
    payload = jnp.concatenate([hidden, extra.astype(jnp.bfloat16)], axis=0)
    spread = lax.all_to_all(
        jnp.broadcast_to(payload[None], (n_tp,) + payload.shape), "tp", 0, 0
    )
    normed = normalise(spread, rows)
    folded = [w_out[0, i * depth : (i + 1) * depth] for i in range(part // span)]
    w_out_mine, payload = lax.optimization_barrier((jnp.concatenate(folded, axis=1), payload))
    packed = lax.all_gather(w_out_mine, "ctx", axis=0, tiled=False)

    local_rows = jnp.arange(rows, dtype=jnp.int32)
    query_pos = positions_of(me * rows + local_rows, stretch_order, block)
    cosine, sine = turning(query_pos)
    query_pos = query_pos[None, :]

    def starts_of(turns):
        stored = jnp.stack([2 * ((me - turn) % n_ctx) + i for turn in turns for i in range(2)])
        return positions_of(stored * block, stretch_order, block)

    keys_values = project(
        key_value_kernel, (rows, 2 * HD), 2 * HD, part, normed, cosine, sine, w_all
    )
    after, _ = lax.optimization_barrier((normed, keys_values))
    query = project(
        query_kernel, (heads, rows, HD), part, 0, after, cosine, sine, w_all
    )
    state = (
        jnp.full((heads, 1, rows), LOW, jnp.float32),
        jnp.zeros((heads, 1, rows), jnp.float32),
        jnp.zeros((heads, HD, rows), jnp.float32),
    )
    half = n_ctx // 2
    up = down = keys_values
    held, turns = [keys_values], [0]
    for turn in range(1, half + 1):
        up = passed_along(up, "ctx", 1)
        if turn < half:
            down = passed_along(down, "ctx", -1)
        state = attend(starts_of(turns), query, query_pos, state, held)
        up, state = lax.optimization_barrier((up, state))
        held, turns = ([up, down], [turn, -turn]) if turn < half else ([up], [turn])
    state = attend(starts_of(turns), query, query_pos, state, held)
    terms = project_out(state[1], state[2], packed, n_tp)
    parts = lax.all_to_all(terms, "tp", 0, 0)
    summed = jnp.sum(parts.astype(jnp.float32), axis=0)
    result = (hidden.astype(jnp.float32) + summed).astype(jnp.bfloat16)[None]
    return passed_along(result, "pipe", 1)


def solution(mesh):
    in_specs = (
        P("pipe", "ctx", "tp"),
        P(),
        P("pipe", "tp"),
        P("pipe", "ctx", "tp"),
        P("pipe", "ctx", "tp"),
        P("pipe", "ctx", "tp"),
        P("pipe", "tp", "ctx"),
    )
    out_specs = P("pipe", "ctx", "tp")
    return jax.shard_map(shards, mesh=mesh, in_specs=in_specs, out_specs=out_specs, check_vma=False)
```

```python
import functools

import jax
import jax.numpy as jnp
from jax import lax
from jax.experimental import pallas as pl
from jax.experimental.pallas import tpu as pltpu
from jax.sharding import PartitionSpec as P

HD = 128


EPS = 1e-05
THETA = 500000.0


def passed_along(value, axis, by):
    length = lax.axis_size(axis)
    return lax.ppermute(value, axis, [(i, (i + by) % length) for i in range(length)])


def turning(pos):
    half = HD // 2
    index = jnp.arange(half, dtype=jnp.float32)
    freq = THETA ** (-2.0 * index / HD)
    angle = pos.astype(jnp.float32)[:, None] * freq[None, :]
    cosine = jnp.cos(angle)
    sine = jnp.sin(angle)
    return jnp.concatenate([cosine, cosine], axis=1), jnp.concatenate([-sine, sine], axis=1)


def passed_on(value, by):
    n_pipe, n_ctx = lax.axis_size("pipe"), lax.axis_size("ctx")
    pairs = [
        (p * n_ctx + c, (p + 1) % n_pipe * n_ctx + (c + by) % n_ctx)
        for p in range(n_pipe)
        for c in range(n_ctx)
    ]
    return lax.ppermute(value, ("pipe", "ctx"), pairs)


def positions_of(stored, stretch_order, block):
    which = stored // block
    slots = jnp.arange(stretch_order.shape[0], dtype=jnp.int32)
    picked = jnp.sum(jnp.where(which[:, None] == slots[None, :], stretch_order[None, :], 0), axis=1)
    return picked * block + stored % block


LOW = -1e20
MASKED = -1e30
MIB = 1024 * 1024
ATTENDED = (3, 4, 5, 6, 7, 8)


def normalise_kernel(spread_ref, out_ref):
    n_tp = spread_ref.shape[0]
    rows = out_ref.shape[0]
    part = out_ref.shape[1] // n_tp
    squares = jnp.zeros((rows, 1), jnp.float32)
    for i in range(n_tp):
        values = spread_ref[i, :rows, :].astype(jnp.float32)
        squares = squares + jnp.sum(values * values, axis=1, keepdims=True)
    factor = lax.rsqrt(squares / out_ref.shape[1] + EPS)
    for i in range(n_tp):
        values = spread_ref[i, :rows, :].astype(jnp.float32)
        terms = spread_ref[i, rows:, :].astype(jnp.float32)
        gain = terms[0:1] + terms[1:2] + terms[2:3]
        out_ref[:, i * part : (i + 1) * part] = (values * factor * gain).astype(out_ref.dtype)


def normalise(spread, rows):
    n_tp, _, part = spread.shape
    vmem = pl.BlockSpec(memory_space=pltpu.VMEM)
    return pl.pallas_call(
        normalise_kernel,
        out_shape=jax.ShapeDtypeStruct((rows, n_tp * part), jnp.bfloat16),
        in_specs=[vmem],
        out_specs=vmem,
        compiler_params=pltpu.CompilerParams(vmem_limit_bytes=16 * MIB),
        cost_estimate=pl.CostEstimate(
            flops=6 * rows * n_tp * part, bytes_accessed=4 * rows * n_tp * part, transcendentals=rows
        ),
    )(spread)


def rotated(raw, cosine, sine):
    half = raw.shape[1] // 2
    swapped = jnp.concatenate([raw[:, half:], raw[:, :half]], axis=1)
    return raw * cosine + swapped * sine


def key_value_kernel(normed_ref, cosine_ref, sine_ref, weights_ref, out_ref):
    total = jnp.dot(normed_ref[...], weights_ref[...], preferred_element_type=jnp.float32)
    key = rotated(total[:, :HD], cosine_ref[...], sine_ref[...])
    out_ref[:, :HD] = key.astype(out_ref.dtype)
    out_ref[:, HD:] = total[:, HD:].astype(out_ref.dtype)


def query_kernel(normed_ref, cosine_ref, sine_ref, weights_ref, keys_values_ref, out_ref):
    total = jnp.dot(normed_ref[...], weights_ref[...], preferred_element_type=jnp.float32)
    cosine, sine = cosine_ref[...], sine_ref[...]
    skip = keys_values_ref.shape[1]
    out_ref[:, :skip] = keys_values_ref[...]
    for at in range(0, total.shape[1], HD):
        raw = total[:, at : at + HD]
        out_ref[:, skip + at : skip + at + HD] = rotated(raw, cosine, sine).astype(out_ref.dtype)


def project(kernel, wide, normed, cosine, sine, weights, *extras):
    rows, width = normed.shape
    vmem = pl.BlockSpec(memory_space=pltpu.VMEM)
    return pl.pallas_call(
        kernel,
        out_shape=jax.ShapeDtypeStruct((rows, wide), jnp.bfloat16),
        in_specs=[vmem] * (4 + len(extras)),
        out_specs=vmem,
        compiler_params=pltpu.CompilerParams(vmem_limit_bytes=16 * MIB),
        cost_estimate=pl.CostEstimate(
            flops=2 * rows * width * weights.shape[1],
            bytes_accessed=2 * width * weights.shape[1],
            transcendentals=0,
        ),
    )(normed, cosine, sine, weights, *extras)


def attended(starts_ref, query_ref, query_pos_ref, state, held):
    peak_ref, total_ref, accum_ref = state
    heads, size, rows = accum_ref.shape
    block = rows // 2
    rate = 1.4426950408889634 / size**0.5
    query_pos = query_pos_ref[...]
    within = lax.broadcasted_iota(jnp.int32, (block, rows), 0)
    key = jnp.concatenate([ref[:, :size] for ref in held], axis=0)
    value = jnp.concatenate([ref[:, size : 2 * size] for ref in held], axis=0).T
    allowed = jnp.concatenate(
        [within + starts_ref[i] <= query_pos for i in range(2 * len(held))], axis=0
    )
    scores = [
        jnp.where(
            allowed,
            lax.dot_general(
                key,
                query_ref[:, (head + 2) * size : (head + 3) * size],
                (((1,), (1,)), ((), ())),
                preferred_element_type=jnp.float32,
            ),
            MASKED,
        )
        for head in range(heads)
    ]
    results = []
    for head in range(heads):
        peak = peak_ref[head]
        new_peak = jnp.maximum(peak, jnp.max(scores[head], axis=0, keepdims=True))
        probs = jnp.exp2((scores[head] - new_peak) * rate)
        fade = jnp.exp2((peak - new_peak) * rate)
        mixed = jnp.dot(value, probs.astype(jnp.bfloat16), preferred_element_type=jnp.float32)
        total = total_ref[head] * fade + jnp.sum(probs, axis=0, keepdims=True)
        results.append((new_peak, total, accum_ref[head] * fade + mixed))
    return results


def attend_kernel(starts_ref, query_ref, query_pos_ref, peak_ref, total_ref, accum_ref, *refs):
    new_peak_ref, new_total_ref, new_accum_ref = refs[-3:]
    results = attended(
        starts_ref, query_ref, query_pos_ref, (peak_ref, total_ref, accum_ref), refs[:-3]
    )
    for head, (peak, total, accum) in enumerate(results):
        new_peak_ref[head] = peak
        new_total_ref[head] = total
        new_accum_ref[head] = accum


def attend(starts, query, query_pos, state, held):
    heads, _, rows = state[2].shape
    keys = rows * len(held)
    vmem = pl.BlockSpec(memory_space=pltpu.VMEM)
    return pl.pallas_call(
        attend_kernel,
        out_shape=[jax.ShapeDtypeStruct(part.shape, part.dtype) for part in state],
        in_specs=[pl.BlockSpec(memory_space=pltpu.SMEM)] + [vmem] * (5 + len(held)),
        out_specs=[vmem] * 3,
        compiler_params=pltpu.CompilerParams(vmem_limit_bytes=16 * MIB),
        cost_estimate=pl.CostEstimate(
            flops=4 * heads * rows * HD * keys,
            bytes_accessed=4 * HD * keys,
            transcendentals=heads * rows * keys,
        ),
    )(starts, query, query_pos, *state, *held)


def finish_kernel(starts_ref, query_ref, query_pos_ref, peak_ref, total_ref, accum_ref, *refs):
    weights_ref, out_ref, context_ref = refs[-3:]
    blocks, depth, packed = weights_ref.shape
    size = accum_ref.shape[1]
    per = out_ref.shape[0] * out_ref.shape[2] // blocks
    share = out_ref.shape[2] // per

    @pl.when(pl.program_id(0) == 0)
    def _():
        results = attended(
            starts_ref, query_ref, query_pos_ref, (peak_ref, total_ref, accum_ref), refs[:-3]
        )
        for head, (_, total, accum) in enumerate(results):
            context = (accum / total).T
            context_ref[:, head * size : (head + 1) * size] = context.astype(context_ref.dtype)

    for at in range(blocks):
        total = None
        for i in range(packed // per):
            term = jnp.dot(
                context_ref[:, i * depth : (i + 1) * depth],
                weights_ref[at, :, i * per : (i + 1) * per],
                preferred_element_type=jnp.float32,
            )
            total = term if total is None else total + term
        column = (at % share) * per
        out_ref[at // share, :, column : column + per] = total.astype(out_ref.dtype)


def finish(starts, query, query_pos, state, held, packed, n_tp):
    heads, size, rows = state[2].shape
    n_ctx, deep, wide = packed.shape
    part = heads * size
    steps = 4
    whole = [query, query_pos, *state, *held]
    return pl.pallas_call(
        finish_kernel,
        grid=(steps,),
        out_shape=jax.ShapeDtypeStruct((n_tp, rows, part), jnp.bfloat16),
        in_specs=[pl.BlockSpec(memory_space=pltpu.SMEM)]
        + [pl.BlockSpec(memory_space=pltpu.VMEM)] * len(whole)
        + [pl.BlockSpec((n_ctx // steps, deep, wide), lambda k: (k, 0, 0))],
        out_specs=pl.BlockSpec((n_tp // steps, rows, part), lambda k: (k, 0, 0)),
        scratch_shapes=[pltpu.VMEM((rows, part), jnp.bfloat16)],
        compiler_params=pltpu.CompilerParams(
            dimension_semantics=("arbitrary",), vmem_limit_bytes=16 * MIB
        ),
        cost_estimate=pl.CostEstimate(
            flops=2 * rows * part * part * n_tp,
            bytes_accessed=4 * part * part * n_tp,
            transcendentals=0,
        ),
    )(starts, *whole, packed)


def shards(section_in, stretch_order, norm_gain, w_query, w_key, w_value, w_out):
    hidden = section_in[0]
    rows, part = hidden.shape
    block = rows // 2
    n_ctx = lax.axis_size("ctx")
    n_tp = lax.axis_size("tp")
    me = lax.axis_index("ctx")
    heads = w_query.shape[2] // HD
    depth = w_query.shape[1]
    span = w_out.shape[2]
    w_mine = jnp.concatenate([w_query[0], w_key[0], w_value[0]], axis=1)
    w_all = lax.all_gather(w_mine, "ctx", axis=0, tiled=True)
    folded = [w_out[0, i * depth : (i + 1) * depth] for i in range(part // span)]
    ahead = jnp.concatenate([hidden, jnp.concatenate(folded, axis=1)], axis=0)
    ahead = passed_along(ahead, "pipe", 1)
    residual = ahead[:rows]
    packed = lax.all_gather(ahead[rows:], "ctx", axis=0, tiled=False)
    gain = norm_gain[0]
    high = lax.reduce_precision(gain, 8, 7)
    middle = lax.reduce_precision(gain - high, 8, 7)
    low = gain - high - middle
    extra = jnp.zeros((16, part), jnp.float32)
    extra = extra.at[0].set(high).at[1].set(middle).at[2].set(low)
    payload = jnp.concatenate([hidden, extra.astype(jnp.bfloat16)], axis=0)
    spread = lax.all_to_all(
        jnp.broadcast_to(payload[None], (n_tp,) + payload.shape), "tp", 0, 0
    )
    normed = normalise(spread, rows)
    local_rows = jnp.arange(rows, dtype=jnp.int32)
    query_pos = positions_of(me * rows + local_rows, stretch_order, block)
    cosine, sine = turning(query_pos)
    query_pos = query_pos[None, :]

    def starts_of(turns):
        stored = jnp.stack(
            [2 * ((me - turn) % n_ctx) + i for turn in turns for i in range(2)]
        )
        return positions_of(stored * block, stretch_order, block)

    keys_values = project(key_value_kernel, 2 * HD, normed, cosine, sine, w_all[:, part:])
    w_all, _ = lax.optimization_barrier((w_all, keys_values))
    own = project(
        query_kernel, 2 * HD + part, normed, cosine, sine, w_all[:, :part], keys_values
    )
    state = (
        jnp.full((heads, 1, rows), LOW, jnp.float32),
        jnp.zeros((heads, 1, rows), jnp.float32),
        jnp.zeros((heads, HD, rows), jnp.float32),
    )
    half = n_ctx // 2
    arrived = {}
    waiting = []
    for turn in range(1, half + 1):
        if turn == 1:
            up, down = passed_on(keys_values, 1), passed_on(keys_values, -1)
        else:
            up = passed_along(up, "ctx", 1)
            if turn < half:
                down = passed_along(down, "ctx", -1)
        if turn == 1:
            own, down = lax.optimization_barrier((own, down))
            own = passed_along(own, "pipe", 1)
            arrived[0] = own
            waiting.append(0)
        if turn in ATTENDED:
            state = attend(
                starts_of(waiting), own, query_pos, state, [arrived[t] for t in waiting]
            )
            up, state = lax.optimization_barrier((up, state))
            waiting = []
        arrived[turn], arrived[-turn] = up, down
        waiting += [turn, -turn] if turn < half else [turn]
    terms = finish(
        starts_of(waiting), own, query_pos, state, [arrived[t] for t in waiting], packed, n_tp
    )
    parts = lax.all_to_all(terms, "tp", 0, 0)
    summed = jnp.sum(parts.astype(jnp.float32), axis=0)
    return (residual.astype(jnp.float32) + summed).astype(jnp.bfloat16)[None]


def solution(mesh):
    in_specs = (
        P("pipe", "ctx", "tp"),
        P(),
        P("pipe", "tp"),
        P("pipe", "ctx", "tp"),
        P("pipe", "ctx", "tp"),
        P("pipe", "ctx", "tp"),
        P("pipe", "tp", "ctx"),
    )
    out_specs = P("pipe", "ctx", "tp")
    return jax.shard_map(shards, mesh=mesh, in_specs=in_specs, out_specs=out_specs, check_vma=False)
```

```python
import functools

import jax
import jax.numpy as jnp
from jax import lax
from jax.experimental import pallas as pl
from jax.experimental.pallas import tpu as pltpu
from jax.sharding import PartitionSpec as P

HD = 128


EPS = 1e-05
THETA = 500000.0


def passed_along(value, axis, by):
    length = lax.axis_size(axis)
    return lax.ppermute(value, axis, [(i, (i + by) % length) for i in range(length)])


def turning(pos):
    half = HD // 2
    index = jnp.arange(half, dtype=jnp.float32)
    freq = THETA ** (-2.0 * index / HD)
    angle = pos.astype(jnp.float32)[:, None] * freq[None, :]
    cosine = jnp.cos(angle)
    sine = jnp.sin(angle)
    return jnp.concatenate([cosine, cosine], axis=1), jnp.concatenate([-sine, sine], axis=1)


def way(pipe):
    return 1 - 2 * (pipe % 2)


def round_ctx(value, by, hop):
    n_pipe, n_ctx = lax.axis_size("pipe"), lax.axis_size("ctx")
    pairs = []
    for pipe in range(n_pipe):
        to = (pipe + hop) % n_pipe
        for ctx in range(n_ctx):
            pairs.append((pipe * n_ctx + ctx, to * n_ctx + (ctx + by * way(to)) % n_ctx))
    return lax.ppermute(value, ("pipe", "ctx"), pairs)


def positions_of(stored, stretch_order, block):
    which = stored // block
    slots = jnp.arange(stretch_order.shape[0], dtype=jnp.int32)
    picked = jnp.sum(jnp.where(which[:, None] == slots[None, :], stretch_order[None, :], 0), axis=1)
    return picked * block + stored % block


LOW = -1e20
MASKED = -1e30
MIB = 1024 * 1024
ATTENDED = (3, 4, 5, 6, 7, 8)


def normalise_kernel(spread_ref, out_ref):
    n_tp = spread_ref.shape[0]
    rows = out_ref.shape[0]
    part = out_ref.shape[1] // n_tp
    squares = jnp.zeros((rows, 1), jnp.float32)
    for i in range(n_tp):
        values = spread_ref[i, :rows, :].astype(jnp.float32)
        squares = squares + jnp.sum(values * values, axis=1, keepdims=True)
    factor = lax.rsqrt(squares / out_ref.shape[1] + EPS)
    for i in range(n_tp):
        values = spread_ref[i, :rows, :].astype(jnp.float32)
        terms = spread_ref[i, rows:, :].astype(jnp.float32)
        gain = terms[0:1] + terms[1:2] + terms[2:3]
        out_ref[:, i * part : (i + 1) * part] = (values * factor * gain).astype(out_ref.dtype)


def normalise(spread, rows):
    n_tp, _, part = spread.shape
    vmem = pl.BlockSpec(memory_space=pltpu.VMEM)
    return pl.pallas_call(
        normalise_kernel,
        out_shape=jax.ShapeDtypeStruct((rows, n_tp * part), jnp.bfloat16),
        in_specs=[vmem],
        out_specs=vmem,
        compiler_params=pltpu.CompilerParams(vmem_limit_bytes=16 * MIB),
        cost_estimate=pl.CostEstimate(
            flops=6 * rows * n_tp * part, bytes_accessed=4 * rows * n_tp * part, transcendentals=rows
        ),
    )(spread)


def rotated(raw, cosine, sine):
    half = raw.shape[1] // 2
    swapped = jnp.concatenate([raw[:, half:], raw[:, :half]], axis=1)
    return raw * cosine + swapped * sine


def key_value_kernel(normed_ref, cosine_ref, sine_ref, weights_ref, out_ref):
    total = jnp.dot(normed_ref[...], weights_ref[...], preferred_element_type=jnp.float32)
    key = rotated(total[:, :HD], cosine_ref[...], sine_ref[...])
    out_ref[:, :HD] = key.astype(out_ref.dtype)
    out_ref[:, HD:] = total[:, HD:].astype(out_ref.dtype)


def query_kernel(normed_ref, cosine_ref, sine_ref, weights_ref, keys_values_ref, out_ref):
    total = jnp.dot(normed_ref[...], weights_ref[...], preferred_element_type=jnp.float32)
    cosine, sine = cosine_ref[...], sine_ref[...]
    skip = keys_values_ref.shape[1]
    out_ref[:, :skip] = keys_values_ref[...]
    for at in range(0, total.shape[1], HD):
        raw = total[:, at : at + HD]
        out_ref[:, skip + at : skip + at + HD] = rotated(raw, cosine, sine).astype(out_ref.dtype)


def project(kernel, wide, normed, cosine, sine, weights, *extras):
    rows, width = normed.shape
    vmem = pl.BlockSpec(memory_space=pltpu.VMEM)
    return pl.pallas_call(
        kernel,
        out_shape=jax.ShapeDtypeStruct((rows, wide), jnp.bfloat16),
        in_specs=[vmem] * (4 + len(extras)),
        out_specs=vmem,
        compiler_params=pltpu.CompilerParams(vmem_limit_bytes=16 * MIB),
        cost_estimate=pl.CostEstimate(
            flops=2 * rows * width * weights.shape[1],
            bytes_accessed=2 * width * weights.shape[1],
            transcendentals=0,
        ),
    )(normed, cosine, sine, weights, *extras)


def attended(starts_ref, query_ref, query_pos_ref, state, held):
    peak_ref, total_ref, accum_ref = state
    heads, size, rows = accum_ref.shape
    block = rows // 2
    rate = 1.4426950408889634 / size**0.5
    query_pos = query_pos_ref[...]
    within = lax.broadcasted_iota(jnp.int32, (block, rows), 0)
    key = jnp.concatenate([ref[:, :size] for ref in held], axis=0)
    value = jnp.concatenate([ref[:, size : 2 * size] for ref in held], axis=0).T
    allowed = jnp.concatenate(
        [within + starts_ref[i] <= query_pos for i in range(2 * len(held))], axis=0
    )
    scores = [
        jnp.where(
            allowed,
            lax.dot_general(
                key,
                query_ref[:, (head + 2) * size : (head + 3) * size],
                (((1,), (1,)), ((), ())),
                preferred_element_type=jnp.float32,
            ),
            MASKED,
        )
        for head in range(heads)
    ]
    results = []
    for head in range(heads):
        peak = peak_ref[head]
        new_peak = jnp.maximum(peak, jnp.max(scores[head], axis=0, keepdims=True))
        probs = jnp.exp2((scores[head] - new_peak) * rate)
        fade = jnp.exp2((peak - new_peak) * rate)
        mixed = jnp.dot(value, probs.astype(jnp.bfloat16), preferred_element_type=jnp.float32)
        total = total_ref[head] * fade + jnp.sum(probs, axis=0, keepdims=True)
        results.append((new_peak, total, accum_ref[head] * fade + mixed))
    return results


def attend_kernel(starts_ref, query_ref, query_pos_ref, peak_ref, total_ref, accum_ref, *refs):
    new_peak_ref, new_total_ref, new_accum_ref = refs[-3:]
    results = attended(
        starts_ref, query_ref, query_pos_ref, (peak_ref, total_ref, accum_ref), refs[:-3]
    )
    for head, (peak, total, accum) in enumerate(results):
        new_peak_ref[head] = peak
        new_total_ref[head] = total
        new_accum_ref[head] = accum


def attend(starts, query, query_pos, state, held):
    heads, _, rows = state[2].shape
    keys = rows * len(held)
    vmem = pl.BlockSpec(memory_space=pltpu.VMEM)
    return pl.pallas_call(
        attend_kernel,
        out_shape=[jax.ShapeDtypeStruct(part.shape, part.dtype) for part in state],
        in_specs=[pl.BlockSpec(memory_space=pltpu.SMEM)] + [vmem] * (5 + len(held)),
        out_specs=[vmem] * 3,
        compiler_params=pltpu.CompilerParams(vmem_limit_bytes=16 * MIB),
        cost_estimate=pl.CostEstimate(
            flops=4 * heads * rows * HD * keys,
            bytes_accessed=4 * HD * keys,
            transcendentals=heads * rows * keys,
        ),
    )(starts, query, query_pos, *state, *held)


def finish_kernel(starts_ref, query_ref, query_pos_ref, peak_ref, total_ref, accum_ref, *refs):
    weights_ref, out_ref, context_ref = refs[-3:]
    blocks, depth, packed = weights_ref.shape
    size = accum_ref.shape[1]
    per = out_ref.shape[0] * out_ref.shape[2] // blocks
    share = out_ref.shape[2] // per

    @pl.when(pl.program_id(0) == 0)
    def _():
        results = attended(
            starts_ref, query_ref, query_pos_ref, (peak_ref, total_ref, accum_ref), refs[:-3]
        )
        for head, (_, total, accum) in enumerate(results):
            context = (accum / total).T
            context_ref[:, head * size : (head + 1) * size] = context.astype(context_ref.dtype)

    for at in range(blocks):
        total = None
        for i in range(packed // per):
            term = jnp.dot(
                context_ref[:, i * depth : (i + 1) * depth],
                weights_ref[at, :, i * per : (i + 1) * per],
                preferred_element_type=jnp.float32,
            )
            total = term if total is None else total + term
        column = (at % share) * per
        out_ref[at // share, :, column : column + per] = total.astype(out_ref.dtype)


def finish(starts, query, query_pos, state, held, packed, n_tp):
    heads, size, rows = state[2].shape
    n_ctx, deep, wide = packed.shape
    part = heads * size
    steps = 4
    whole = [query, query_pos, *state, *held]
    return pl.pallas_call(
        finish_kernel,
        grid=(steps,),
        out_shape=jax.ShapeDtypeStruct((n_tp, rows, part), jnp.bfloat16),
        in_specs=[pl.BlockSpec(memory_space=pltpu.SMEM)]
        + [pl.BlockSpec(memory_space=pltpu.VMEM)] * len(whole)
        + [pl.BlockSpec((n_ctx // steps, deep, wide), lambda k: (k, 0, 0))],
        out_specs=pl.BlockSpec((n_tp // steps, rows, part), lambda k: (k, 0, 0)),
        scratch_shapes=[pltpu.VMEM((rows, part), jnp.bfloat16)],
        compiler_params=pltpu.CompilerParams(
            dimension_semantics=("arbitrary",), vmem_limit_bytes=16 * MIB
        ),
        cost_estimate=pl.CostEstimate(
            flops=2 * rows * part * part * n_tp,
            bytes_accessed=4 * part * part * n_tp,
            transcendentals=0,
        ),
    )(starts, *whole, packed)


def shards(section_in, stretch_order, norm_gain, w_query, w_key, w_value, w_out):
    hidden = section_in[0]
    rows, part = hidden.shape
    block = rows // 2
    n_ctx = lax.axis_size("ctx")
    n_tp = lax.axis_size("tp")
    me = lax.axis_index("ctx")
    heads = w_query.shape[2] // HD
    depth = w_query.shape[1]
    span = w_out.shape[2]
    w_mine = jnp.concatenate([w_query[0], w_key[0], w_value[0]], axis=1)
    w_all = lax.all_gather(w_mine, "ctx", axis=0, tiled=True)
    folded = [w_out[0, i * depth : (i + 1) * depth] for i in range(part // span)]
    ahead = jnp.concatenate([hidden, jnp.concatenate(folded, axis=1)], axis=0)
    ahead = passed_along(ahead, "pipe", 1)
    residual = ahead[:rows]
    packed = lax.all_gather(ahead[rows:], "ctx", axis=0, tiled=False)
    gain = norm_gain[0]
    high = lax.reduce_precision(gain, 8, 7)
    middle = lax.reduce_precision(gain - high, 8, 7)
    low = gain - high - middle
    extra = jnp.zeros((16, part), jnp.float32)
    extra = extra.at[0].set(high).at[1].set(middle).at[2].set(low)
    payload = jnp.concatenate([hidden, extra.astype(jnp.bfloat16)], axis=0)
    spread = lax.all_to_all(
        jnp.broadcast_to(payload[None], (n_tp,) + payload.shape), "tp", 0, 0
    )
    normed = normalise(spread, rows)
    local_rows = jnp.arange(rows, dtype=jnp.int32)
    query_pos = positions_of(me * rows + local_rows, stretch_order, block)
    cosine, sine = turning(query_pos)
    query_pos = query_pos[None, :]

    sense = way(lax.axis_index("pipe"))

    def starts_of(turns):
        stored = jnp.stack(
            [2 * ((me - turn * sense) % n_ctx) + i for turn in turns for i in range(2)]
        )
        return positions_of(stored * block, stretch_order, block)

    keys_values = project(key_value_kernel, 2 * HD, normed, cosine, sine, w_all[:, part:])
    w_all, _ = lax.optimization_barrier((w_all, keys_values))
    own = project(
        query_kernel, 2 * HD + part, normed, cosine, sine, w_all[:, :part], keys_values
    )
    state = (
        jnp.full((heads, 1, rows), LOW, jnp.float32),
        jnp.zeros((heads, 1, rows), jnp.float32),
        jnp.zeros((heads, HD, rows), jnp.float32),
    )
    half = n_ctx // 2
    arrived = {}
    waiting = []
    for turn in range(1, half + 1):
        if turn == 1:
            up, down = round_ctx(keys_values, 1, 1), round_ctx(keys_values, -1, 1)
        else:
            up = round_ctx(up, 1, 0)
            if turn < half:
                down = round_ctx(down, -1, 0)
        if turn == 1:
            own, down = lax.optimization_barrier((own, down))
            own = passed_along(own, "pipe", 1)
            arrived[0] = own
            waiting.append(0)
        if turn in ATTENDED:
            state = attend(
                starts_of(waiting), own, query_pos, state, [arrived[t] for t in waiting]
            )
            up, state = lax.optimization_barrier((up, state))
            waiting = []
        arrived[turn], arrived[-turn] = up, down
        waiting += [turn, -turn] if turn < half else [turn]
    terms = finish(
        starts_of(waiting), own, query_pos, state, [arrived[t] for t in waiting], packed, n_tp
    )
    parts = lax.all_to_all(terms, "tp", 0, 0)
    summed = jnp.sum(parts.astype(jnp.float32), axis=0)
    return (residual.astype(jnp.float32) + summed).astype(jnp.bfloat16)[None]


def solution(mesh):
    in_specs = (
        P("pipe", "ctx", "tp"),
        P(),
        P("pipe", "tp"),
        P("pipe", "ctx", "tp"),
        P("pipe", "ctx", "tp"),
        P("pipe", "ctx", "tp"),
        P("pipe", "tp", "ctx"),
    )
    out_specs = P("pipe", "ctx", "tp")
    return jax.shard_map(shards, mesh=mesh, in_specs=in_specs, out_specs=out_specs, check_vma=False)
```

```python
import functools

import jax
import jax.numpy as jnp
from jax import lax
from jax.experimental import pallas as pl
from jax.experimental.pallas import tpu as pltpu
from jax.sharding import PartitionSpec as P

HD = 128


EPS = 1e-05
THETA = 500000.0


def passed_along(value, axis, by):
    length = lax.axis_size(axis)
    return lax.ppermute(value, axis, [(i, (i + by) % length) for i in range(length)])


def turning(pos):
    half = HD // 2
    index = jnp.arange(half, dtype=jnp.float32)
    freq = THETA ** (-2.0 * index / HD)
    angle = pos.astype(jnp.float32)[:, None] * freq[None, :]
    cosine = jnp.cos(angle)
    sine = jnp.sin(angle)
    return jnp.concatenate([cosine, cosine], axis=1), jnp.concatenate([-sine, sine], axis=1)


def way(pipe):
    return 1 - 2 * (pipe % 2)


def round_ctx(value, by, hop):
    n_pipe, n_ctx = lax.axis_size("pipe"), lax.axis_size("ctx")
    pairs = []
    for pipe in range(n_pipe):
        to = (pipe + hop) % n_pipe
        for ctx in range(n_ctx):
            pairs.append((pipe * n_ctx + ctx, to * n_ctx + (ctx + by * way(to)) % n_ctx))
    return lax.ppermute(value, ("pipe", "ctx"), pairs)


def positions_of(stored, stretch_order, block):
    which = stored // block
    slots = jnp.arange(stretch_order.shape[0], dtype=jnp.int32)
    picked = jnp.sum(jnp.where(which[:, None] == slots[None, :], stretch_order[None, :], 0), axis=1)
    return picked * block + stored % block


LOW = -1e20
MASKED = -1e30
MIB = 1024 * 1024
ATTENDED = (3, 4, 5, 6, 7, 8)


def normalise_kernel(spread_ref, out_ref):
    n_tp = spread_ref.shape[0]
    rows = out_ref.shape[0]
    part = out_ref.shape[1] // n_tp
    squares = jnp.zeros((rows, 1), jnp.float32)
    for i in range(n_tp):
        values = spread_ref[i, :rows, :].astype(jnp.float32)
        squares = squares + jnp.sum(values * values, axis=1, keepdims=True)
    factor = lax.rsqrt(squares / out_ref.shape[1] + EPS)
    for i in range(n_tp):
        values = spread_ref[i, :rows, :].astype(jnp.float32)
        terms = spread_ref[i, rows:, :].astype(jnp.float32)
        gain = terms[0:1] + terms[1:2] + terms[2:3]
        out_ref[:, i * part : (i + 1) * part] = (values * factor * gain).astype(out_ref.dtype)


def normalise(spread, rows):
    n_tp, _, part = spread.shape
    vmem = pl.BlockSpec(memory_space=pltpu.VMEM)
    return pl.pallas_call(
        normalise_kernel,
        out_shape=jax.ShapeDtypeStruct((rows, n_tp * part), jnp.bfloat16),
        in_specs=[vmem],
        out_specs=vmem,
        compiler_params=pltpu.CompilerParams(vmem_limit_bytes=16 * MIB),
        cost_estimate=pl.CostEstimate(
            flops=6 * rows * n_tp * part, bytes_accessed=4 * rows * n_tp * part, transcendentals=rows
        ),
    )(spread)


def rotated(raw, cosine, sine):
    half = raw.shape[1] // 2
    swapped = jnp.concatenate([raw[:, half:], raw[:, :half]], axis=1)
    return raw * cosine + swapped * sine


def key_value_kernel(normed_ref, cosine_ref, sine_ref, weights_ref, out_ref):
    total = jnp.dot(normed_ref[...], weights_ref[...], preferred_element_type=jnp.float32)
    key = rotated(total[:, :HD], cosine_ref[...], sine_ref[...])
    out_ref[:, :HD] = key.astype(out_ref.dtype)
    out_ref[:, HD:] = total[:, HD:].astype(out_ref.dtype)


def query_kernel(normed_ref, cosine_ref, sine_ref, weights_ref, keys_values_ref, out_ref):
    total = jnp.dot(normed_ref[...], weights_ref[...], preferred_element_type=jnp.float32)
    cosine, sine = cosine_ref[...], sine_ref[...]
    skip = keys_values_ref.shape[1]
    out_ref[:, :skip] = keys_values_ref[...]
    for at in range(0, total.shape[1], HD):
        raw = total[:, at : at + HD]
        out_ref[:, skip + at : skip + at + HD] = rotated(raw, cosine, sine).astype(out_ref.dtype)


def project(kernel, wide, normed, cosine, sine, weights, *extras):
    rows, width = normed.shape
    vmem = pl.BlockSpec(memory_space=pltpu.VMEM)
    return pl.pallas_call(
        kernel,
        out_shape=jax.ShapeDtypeStruct((rows, wide), jnp.bfloat16),
        in_specs=[vmem] * (4 + len(extras)),
        out_specs=vmem,
        compiler_params=pltpu.CompilerParams(vmem_limit_bytes=16 * MIB),
        cost_estimate=pl.CostEstimate(
            flops=2 * rows * width * weights.shape[1],
            bytes_accessed=2 * width * weights.shape[1],
            transcendentals=0,
        ),
    )(normed, cosine, sine, weights, *extras)


def attended(starts_ref, query_ref, query_pos_ref, state, held):
    peak_ref, total_ref, accum_ref = state
    heads, size, rows = accum_ref.shape
    block = rows // 2
    rate = 1.4426950408889634 / size**0.5
    query_pos = query_pos_ref[...]
    within = lax.broadcasted_iota(jnp.int32, (block, rows), 0)
    key = jnp.concatenate([ref[:, :size] for ref in held], axis=0)
    value = jnp.concatenate([ref[:, size : 2 * size] for ref in held], axis=0).T
    allowed = jnp.concatenate(
        [within + starts_ref[i] <= query_pos for i in range(2 * len(held))], axis=0
    )
    scores = [
        jnp.where(
            allowed,
            lax.dot_general(
                key,
                query_ref[:, (head + 2) * size : (head + 3) * size],
                (((1,), (1,)), ((), ())),
                preferred_element_type=jnp.float32,
            ),
            MASKED,
        )
        for head in range(heads)
    ]
    results = []
    for head in range(heads):
        peak = peak_ref[head]
        new_peak = jnp.maximum(peak, jnp.max(scores[head], axis=0, keepdims=True))
        probs = jnp.exp2((scores[head] - new_peak) * rate)
        fade = jnp.exp2((peak - new_peak) * rate)
        mixed = jnp.dot(value, probs.astype(jnp.bfloat16), preferred_element_type=jnp.float32)
        total = total_ref[head] * fade + jnp.sum(probs, axis=0, keepdims=True)
        results.append((new_peak, total, accum_ref[head] * fade + mixed))
    return results


def attend_kernel(starts_ref, query_ref, query_pos_ref, peak_ref, total_ref, accum_ref, *refs):
    new_peak_ref, new_total_ref, new_accum_ref = refs[-3:]
    results = attended(
        starts_ref, query_ref, query_pos_ref, (peak_ref, total_ref, accum_ref), refs[:-3]
    )
    for head, (peak, total, accum) in enumerate(results):
        new_peak_ref[head] = peak
        new_total_ref[head] = total
        new_accum_ref[head] = accum


def attend(starts, query, query_pos, state, held):
    heads, _, rows = state[2].shape
    keys = rows * len(held)
    vmem = pl.BlockSpec(memory_space=pltpu.VMEM)
    return pl.pallas_call(
        attend_kernel,
        out_shape=[jax.ShapeDtypeStruct(part.shape, part.dtype) for part in state],
        in_specs=[pl.BlockSpec(memory_space=pltpu.SMEM)] + [vmem] * (5 + len(held)),
        out_specs=[vmem] * 3,
        compiler_params=pltpu.CompilerParams(vmem_limit_bytes=16 * MIB),
        cost_estimate=pl.CostEstimate(
            flops=4 * heads * rows * HD * keys,
            bytes_accessed=4 * HD * keys,
            transcendentals=heads * rows * keys,
        ),
    )(starts, query, query_pos, *state, *held)


def finish_kernel(starts_ref, query_ref, query_pos_ref, peak_ref, total_ref, accum_ref, *refs):
    weights_ref, even_ref, odd_ref, context_ref = refs[-4:]
    blocks, depth, packed = weights_ref.shape
    size = accum_ref.shape[1]
    per = even_ref.shape[2]

    @pl.when(pl.program_id(0) == 0)
    def _():
        results = attended(
            starts_ref, query_ref, query_pos_ref, (peak_ref, total_ref, accum_ref), refs[:-4]
        )
        for head, (_, total, accum) in enumerate(results):
            context = (accum / total).T
            context_ref[:, head * size : (head + 1) * size] = context.astype(context_ref.dtype)

    for at in range(blocks):
        total = None
        for i in range(packed // per):
            term = jnp.dot(
                context_ref[:, i * depth : (i + 1) * depth],
                weights_ref[at, :, i * per : (i + 1) * per],
                preferred_element_type=jnp.float32,
            )
            total = term if total is None else total + term
        out_ref = odd_ref if at % 2 else even_ref
        out_ref[at // 2] = total.astype(out_ref.dtype)


def finish(starts, query, query_pos, state, held, packed, n_tp):
    heads, size, rows = state[2].shape
    n_ctx, deep, wide = packed.shape
    part = heads * size
    steps = 4
    whole = [query, query_pos, *state, *held]
    return pl.pallas_call(
        finish_kernel,
        grid=(steps,),
        out_shape=[jax.ShapeDtypeStruct((n_tp, rows, part // 2), jnp.bfloat16)] * 2,
        in_specs=[pl.BlockSpec(memory_space=pltpu.SMEM)]
        + [pl.BlockSpec(memory_space=pltpu.VMEM)] * len(whole)
        + [pl.BlockSpec((n_ctx // steps, deep, wide), lambda k: (k, 0, 0))],
        out_specs=[pl.BlockSpec((n_tp // steps, rows, part // 2), lambda k: (k, 0, 0))] * 2,
        scratch_shapes=[pltpu.VMEM((rows, part), jnp.bfloat16)],
        compiler_params=pltpu.CompilerParams(
            dimension_semantics=("arbitrary",), vmem_limit_bytes=16 * MIB
        ),
        cost_estimate=pl.CostEstimate(
            flops=2 * rows * part * part * n_tp,
            bytes_accessed=4 * part * part * n_tp,
            transcendentals=0,
        ),
    )(starts, *whole, packed)


def shards(section_in, stretch_order, norm_gain, w_query, w_key, w_value, w_out):
    hidden = section_in[0]
    rows, part = hidden.shape
    block = rows // 2
    n_ctx = lax.axis_size("ctx")
    n_tp = lax.axis_size("tp")
    me = lax.axis_index("ctx")
    heads = w_query.shape[2] // HD
    depth = w_query.shape[1]
    span = w_out.shape[2]
    w_mine = jnp.concatenate([w_query[0], w_key[0], w_value[0]], axis=1)
    w_all = lax.all_gather(w_mine, "ctx", axis=0, tiled=True)
    folded = [w_out[0, i * depth : (i + 1) * depth] for i in range(part // span)]
    ahead = jnp.concatenate([hidden, jnp.concatenate(folded, axis=1)], axis=0)
    ahead = passed_along(ahead, "pipe", 1)
    residual = ahead[:rows]
    packed = lax.all_gather(ahead[rows:], "ctx", axis=0, tiled=False)
    gain = norm_gain[0]
    high = lax.reduce_precision(gain, 8, 7)
    middle = lax.reduce_precision(gain - high, 8, 7)
    low = gain - high - middle
    extra = jnp.zeros((16, part), jnp.float32)
    extra = extra.at[0].set(high).at[1].set(middle).at[2].set(low)
    payload = jnp.concatenate([hidden, extra.astype(jnp.bfloat16)], axis=0)
    spread = lax.all_to_all(
        jnp.broadcast_to(payload[None], (n_tp,) + payload.shape), "tp", 0, 0
    )
    normed = normalise(spread, rows)
    local_rows = jnp.arange(rows, dtype=jnp.int32)
    query_pos = positions_of(me * rows + local_rows, stretch_order, block)
    cosine, sine = turning(query_pos)
    query_pos = query_pos[None, :]

    sense = way(lax.axis_index("pipe"))

    def starts_of(turns):
        stored = jnp.stack(
            [2 * ((me - turn * sense) % n_ctx) + i for turn in turns for i in range(2)]
        )
        return positions_of(stored * block, stretch_order, block)

    keys_values = project(key_value_kernel, 2 * HD, normed, cosine, sine, w_all[:, part:])
    w_all, _ = lax.optimization_barrier((w_all, keys_values))
    own = project(
        query_kernel, 2 * HD + part, normed, cosine, sine, w_all[:, :part], keys_values
    )
    state = (
        jnp.full((heads, 1, rows), LOW, jnp.float32),
        jnp.zeros((heads, 1, rows), jnp.float32),
        jnp.zeros((heads, HD, rows), jnp.float32),
    )
    half = n_ctx // 2
    arrived = {}
    waiting = []
    for turn in range(1, half + 1):
        if turn == 1:
            up, down = round_ctx(keys_values, 1, 1), round_ctx(keys_values, -1, 1)
        else:
            up = round_ctx(up, 1, 0)
            if turn < half:
                down = round_ctx(down, -1, 0)
        if turn == 1:
            own, down = lax.optimization_barrier((own, down))
            own = passed_along(own, "pipe", 1)
            arrived[0] = own
            waiting.append(0)
        if turn in ATTENDED:
            state = attend(
                starts_of(waiting), own, query_pos, state, [arrived[t] for t in waiting]
            )
            up, state = lax.optimization_barrier((up, state))
            waiting = []
        arrived[turn], arrived[-turn] = up, down
        waiting += [turn, -turn] if turn < half else [turn]
    terms = finish(
        starts_of(waiting), own, query_pos, state, [arrived[t] for t in waiting], packed, n_tp
    )
    parts = [lax.all_to_all(term, "tp", 0, 0) for term in terms]
    summed = jnp.concatenate([jnp.sum(p.astype(jnp.float32), axis=0) for p in parts], axis=1)
    return (residual.astype(jnp.float32) + summed).astype(jnp.bfloat16)[None]


def solution(mesh):
    in_specs = (
        P("pipe", "ctx", "tp"),
        P(),
        P("pipe", "tp"),
        P("pipe", "ctx", "tp"),
        P("pipe", "ctx", "tp"),
        P("pipe", "ctx", "tp"),
        P("pipe", "tp", "ctx"),
    )
    out_specs = P("pipe", "ctx", "tp")
    return jax.shard_map(shards, mesh=mesh, in_specs=in_specs, out_specs=out_specs, check_vma=False)
```
